32 devices in a mesh: ax: 8 (over z, y), az: 2 (over x), rad: 2 (over core).
Axes of the slice: x: 2, y: 2, z: 4, core: 2. Of those that a mesh axis runs over, the one named last changes fastest.
Arguments:
- state: float32 [5, 64, 128, 1024], P(None, 'ax', 'rad', 'az'), may hold values from -6 to 6
- section: float32 [5, 64, 128, 1024], P(None, 'ax', 'rad', 'az'), may hold values from -6 to 6
- mean_axial: float32 [128], P('rad'), may hold values from 0.3 to 0.6
- mean_swirl: float32 [128], P('rad'), may hold values from 0.1 to 0.4
- mean_density: float32 [128], P('rad'), may hold values from 0.8 to 1.25
- sound_squared: float32 [128], P('rad'), may hold values from 0.8 to 1.25
Outputs:
- new_state: float32 [5, 64, 128, 1024], P(None, 'ax', 'rad', 'az')
- new_section: float32 [5, 64, 128, 1024], P(None, 'ax', 'rad', 'az')
The draws below stay inside these ranges and needn't reach their ends.
All inputs are finite; a program needn't handle non-finite values.
Results may differ from the reference program's by a relative error of at most 0.00005.
Values sent between devices are 32-bit elements; how exact they have to be, the bound alone decides.
A program may use at most 128 MiB of HBM per device.

```python
import math
import jax
import jax.numpy as jnp

NT = 1024
NX = 64
NR = 128


def draw_state(key, part):
    first_key = jax.random.fold_in(jax.random.fold_in(key, 11), 0)
    return jnp.clip(jax.random.normal(first_key, (5, NX, NR, NT), jnp.float32), -6.0, 6.0)


def steps_of(own_key, dims, cuts, smallest, largest):
    level, own = 1.0, jax.random.fold_in(own_key, 6)
    for dim, shards_of in cuts:
        steps = jnp.exp(jax.random.uniform(jax.random.fold_in(own, dim), (shards_of,), jnp.float32, smallest / len(cuts), largest / len(cuts)))
        level = level * jnp.repeat(steps, dims[dim] // shards_of).reshape([-1 if axis == dim else 1 for axis in range(len(dims))])
    return level


def scatter_about(rng, extent, scale, limit, cuts=(), kind=jnp.bfloat16):
    loudness = steps_of(rng, extent, cuts, -0.22, 0.18) if cuts else 1.0
    values = jax.random.normal(rng, extent, jnp.float32) * scale * loudness
    return jnp.minimum(jnp.maximum(values, -limit), limit).astype(kind)


def setup_inputs(seed: int = 0) -> dict:
    streams_of = jax.random.split(jax.random.key(seed), 7)
    return {
        "state": draw_state(jax.random.fold_in(streams_of[6], 71), 0),
        "section": scatter_about(streams_of[1], (5, NX, NR, NT), 1.0, 6.0, ((1, 8), (2, 2), (3, 2)), jnp.float32),
        "mean_axial": jnp.clip(0.3 + 0.3 * jax.random.uniform(streams_of[2], (NR,), jnp.float32) ** steps_of(streams_of[2], (NR,), ((0, 2),), -0.2, 0.2), 0.3, 0.6),
        "mean_swirl": jnp.clip(0.1 + 0.3 * jax.random.uniform(streams_of[3], (NR,), jnp.float32) ** steps_of(streams_of[3], (NR,), ((0, 2),), -0.2, 0.2), 0.1, 0.4),
        "mean_density": jnp.clip(0.8 + 0.45 * jax.random.uniform(streams_of[4], (NR,), jnp.float32) ** steps_of(streams_of[4], (NR,), ((0, 2),), -0.2, 0.2), 0.8, 1.25),
        "sound_squared": jnp.clip(0.8 + 0.45 * jax.random.uniform(streams_of[5], (NR,), jnp.float32) ** steps_of(streams_of[5], (NR,), ((0, 2),), -0.2, 0.2), 0.8, 1.25),
    }


drp_coeffs = (0.770882380518, -0.166705904415, 0.020843142770)
section_keep = -0.4178904745
section_gain = 0.3792103129999
time_step = 0.25


def axial_derivative(fields):
    count = fields.shape[1]
    padded = jnp.pad(fields, ((0, 0), (3, 3), (0, 0), (0, 0)))
    result = jnp.zeros_like(fields)
    for offset in range(1, 4):
        upper = padded[:, 3 + offset:3 + offset + count]
        lower = padded[:, 3 - offset:3 - offset + count]
        result = result + drp_coeffs[offset - 1] * (upper - lower)
    return result


def radial_derivative(pair):
    count = pair.shape[2]
    signs = jnp.array([-1.0, 1.0], dtype=jnp.float32).reshape(2, 1, 1, 1)
    lower_wall = signs * jnp.flip(pair[:, :, 0:3], axis=2)
    upper_wall = signs * jnp.flip(pair[:, :, count - 3:count], axis=2)
    padded = jnp.concatenate([lower_wall, pair, upper_wall], axis=2)
    result = jnp.zeros_like(pair)
    for offset in range(1, 4):
        upper = padded[:, :, 3 + offset:3 + offset + count]
        lower = padded[:, :, 3 - offset:3 - offset + count]
        result = result + drp_coeffs[offset - 1] * (upper - lower)
    return result


def azimuthal_derivative(fields):
    spectrum = jnp.fft.rfft(fields, axis=-1)
    modes = jnp.arange(NT // 2 + 1)
    factor = jnp.where(modes == NT // 2, 0, modes).astype(jnp.float32)
    return jnp.fft.irfft(1j * factor * spectrum, n=NT, axis=-1).astype(jnp.float32)


def reference(state, section, mean_axial, mean_swirl, mean_density, sound_squared):
    radius = NT / (2.0 * math.pi) + jnp.arange(NR).astype(jnp.float32) + 0.5
    inv_radius = (1.0 / radius)[:, None]
    axial_speed = mean_axial[:, None]
    swirl_rate = mean_swirl[:, None] * inv_radius
    density = mean_density[:, None]
    inv_density = 1.0 / density
    stiffness = density * sound_squared[:, None]
    axial_grad = axial_derivative(state)
    azim_grad = azimuthal_derivative(state)
    radial_grad = radial_derivative(state[2::2])
    convect = axial_speed * axial_grad + swirl_rate * azim_grad
    diverge = axial_grad[1] + radial_grad[0] + inv_radius * azim_grad[3]
    rhs = jnp.stack([
        -(convect[0] + density * diverge),
        -(convect[1] + axial_grad[4] * inv_density),
        -(convect[2] + radial_grad[1] * inv_density),
        -(convect[3] + inv_radius * azim_grad[4] * inv_density),
        -(convect[4] + stiffness * diverge),
    ])
    new_section = section_keep * section + time_step * rhs
    return state + section_gain * new_section, new_section
```

```python
import functools
import math

import jax
import jax.numpy as jnp
import numpy as np
from jax import lax
from jax.experimental import pallas as pl
from jax.experimental.pallas import tpu as pltpu
from jax.sharding import PartitionSpec as P

NT = 1024
MESH = pl.DeviceIdType.MESH

drp_coeffs = (0.770882380518, -0.166705904415, 0.02084314277)
section_keep = -0.4178904745
section_gain = 0.3792103129999
time_step = 0.25
HALO = 3
RIM = 8


def spectral_tables(owners, local):
    s = np.arange(local)[:, None]
    t = np.arange(local)[None, :]
    tables = []
    for d in range(owners):
        spacing = (t - s + d * local) % NT
        spacing = np.where(spacing > NT // 2, spacing - NT, spacing)
        angle = np.pi * spacing / NT
        safe = np.where(spacing == 0, 1.0, np.sin(angle))
        parity = 1.0 - 2.0 * (spacing % 2)
        tables.append(np.where(spacing == 0, 0.0, 0.5 * parity * np.cos(angle) / safe))
    full = np.stack(tables).astype(np.float32)
    high = full.astype(jnp.bfloat16)
    low = (full - high.astype(np.float32)).astype(jnp.bfloat16)
    return np.stack([high, low], axis=1)


def kernel(
    sizes, state, section, axial_speed, swirl, density_in, sound, table_in, out_state, out_section,
    st, pr, other, ns, nst, coef, table, means,
    load_sem, az_send, az_recv, ax_send, ax_recv, rad_send, rad_recv, out_sem,
):
    n_ax, n_az, n_rad, count, rows, local = sizes
    ax = lax.axis_index("ax")
    az = lax.axis_index("az")
    rad = lax.axis_index("rad")
    has_prev, has_next = ax > 0, ax < n_ax - 1
    has_low, has_high = rad > 0, rad < n_rad - 1

    def az_copy(d, c):
        return pltpu.make_async_remote_copy(
            src_ref=state.at[:, c],
            dst_ref=other.at[d - 1, :, c],
            send_sem=az_send.at[d - 1, c],
            recv_sem=az_recv.at[d - 1, c],
            device_id={"az": lax.rem(az + d, n_az)},
            device_id_type=MESH,
        )

    def ax_copy(up):
        return pltpu.make_async_remote_copy(
            src_ref=state.at[:, pl.ds(count - HALO if up else 0, HALO)],
            dst_ref=st.at[:, pl.ds(0 if up else count + HALO, HALO)],
            send_sem=ax_send.at[0 if up else 1],
            recv_sem=ax_recv.at[0 if up else 1],
            device_id={"ax": ax + 1 if up else ax - 1},
            device_id_type=MESH,
        )

    def rad_copy(up, k):
        return pltpu.make_async_remote_copy(
            src_ref=state.at[2 + 2 * k, :, pl.ds(rows - RIM if up else 0, RIM)],
            dst_ref=pr.at[k, :, pl.ds(0 if up else rows + RIM, RIM)],
            send_sem=rad_send.at[0 if up else 1, k],
            recv_sem=rad_recv.at[0 if up else 1, k],
            device_id={"rad": rad + 1 if up else rad - 1},
            device_id_type=MESH,
        )

    loads = [
        pltpu.make_async_copy(state, st.at[:, pl.ds(HALO, count)], load_sem.at[0]),
        pltpu.make_async_copy(section, ns, load_sem.at[1]),
        pltpu.make_async_copy(state.at[2], pr.at[0, :, pl.ds(RIM, rows)], load_sem.at[2]),
        pltpu.make_async_copy(state.at[4], pr.at[1, :, pl.ds(RIM, rows)], load_sem.at[3]),
        pltpu.make_async_copy(table_in, table, load_sem.at[4]),
    ]
    vectors = [
        pltpu.make_async_copy(ref, means.at[i], load_sem.at[5 + i])
        for i, ref in enumerate((axial_speed, swirl, density_in, sound))
    ]
    for copy in vectors:
        copy.start()

    barrier = pltpu.get_barrier_semaphore()

    def greet(axis, index):
        pl.semaphore_signal(barrier, inc=1, device_id={axis: index}, device_id_type=MESH)

    for d in range(1, n_az):
        greet("az", lax.rem(az + d, n_az))
    pl.when(has_prev)(lambda: greet("ax", ax - 1))
    pl.when(has_next)(lambda: greet("ax", ax + 1))
    pl.when(has_low)(lambda: greet("rad", rad - 1))
    pl.when(has_high)(lambda: greet("rad", rad + 1))
    met = n_az - 1
    for there in (has_prev, has_next, has_low, has_high):
        met = met + there.astype(jnp.int32)
    pl.semaphore_wait(barrier, met)

    def send_plane(c, carry):
        for d in range(1, n_az):
            az_copy(d, c).start()
        return carry

    send_plane(0, 0)
    pl.when(has_next)(lambda: ax_copy(True).start())
    pl.when(has_prev)(lambda: ax_copy(False).start())
    for k in range(2):
        pl.when(has_high)(lambda: rad_copy(True, k).start())
        pl.when(has_low)(lambda: rad_copy(False, k).start())
    lax.fori_loop(1, count, send_plane, 0)
    for copy in loads:
        copy.start()

    for copy in vectors:
        copy.wait()

    pick = lax.broadcasted_iota(jnp.int32, (rows, rows), 0) == lax.broadcasted_iota(
        jnp.int32, (rows, rows), 1
    )

    def column(i):
        line = jnp.broadcast_to(means[i], (rows, rows))
        return jnp.sum(jnp.where(pick, line, 0.0), axis=1, keepdims=True)

    cell = lax.broadcasted_iota(jnp.int32, (rows, local), 0) + rad * rows
    inv_radius = 1.0 / (NT / (2.0 * math.pi) + cell.astype(jnp.float32) + 0.5)
    density = jnp.broadcast_to(column(2), (rows, local))
    minus = -time_step
    inverse = minus / density
    stiff = minus * density * column(3)
    coef[0] = jnp.broadcast_to(minus * column(0), (rows, local))
    coef[1] = minus * column(1) * inv_radius
    coef[2] = minus * density
    coef[3] = stiff
    coef[4] = inverse
    coef[5] = minus * density * inv_radius
    coef[6] = stiff * inv_radius
    coef[7] = inverse * inv_radius

    def azimuthal(values, d):
        flat = values.reshape(5 * rows, local)
        high = flat.astype(jnp.bfloat16)
        low = (flat - high.astype(jnp.float32)).astype(jnp.bfloat16)
        dot = functools.partial(jnp.dot, preferred_element_type=jnp.float32)
        g = dot(high, table[d, 0]) + dot(low, table[d, 0]) + dot(high, table[d, 1])
        return g.reshape(5, rows, local)

    def add_azimuthal(c, g):
        rate = coef[1]
        ns[0, c] += rate * g[0] + coef[5] * g[3]
        ns[1, c] += rate * g[1]
        ns[2, c] += rate * g[2]
        ns[3, c] += rate * g[3] + coef[7] * g[4]
        ns[4, c] += rate * g[4] + coef[6] * g[3]

    def radial(k, c):
        total = jnp.zeros((rows, local), jnp.float32)
        for j in range(1, 4):
            total += drp_coeffs[j - 1] * (
                pr[k, c, pl.ds(RIM + j, rows)] - pr[k, c, pl.ds(RIM - j, rows)]
            )
        return total

    def axial(f, c):
        total = jnp.zeros((rows, local), jnp.float32)
        for j in range(1, 4):
            total += drp_coeffs[j - 1] * (st[f, c + HALO + j] - st[f, c + HALO - j])
        return total

    for copy in loads:
        copy.wait()

    def wall(low):
        def fill(c, carry):
            for k, sign in enumerate((-1.0, 1.0)):
                for j in range(3):
                    if low:
                        pr[k, c, pl.ds(RIM - 1 - j, 1)] = sign * pr[k, c, pl.ds(RIM + j, 1)]
                    else:
                        pr[k, c, pl.ds(RIM + rows + j, 1)] = sign * pr[
                            k, c, pl.ds(RIM + rows - 1 - j, 1)
                        ]
            return carry

        lax.fori_loop(0, count, fill, 0)

    pl.when(jnp.logical_not(has_low))(lambda: wall(True))
    pl.when(jnp.logical_not(has_high))(lambda: wall(False))
    for k in range(2):
        pl.when(has_low)(lambda: rad_copy(True, k).wait_recv())
        pl.when(has_high)(lambda: rad_copy(False, k).wait_recv())

    def own_part(c, carry):
        for f in range(5):
            ns[f, c] = section_keep * ns[f, c]
        spread = radial(0, c)
        ns[0, c] += coef[2] * spread
        ns[4, c] += coef[3] * spread
        ns[2, c] += coef[4] * radial(1, c)
        add_azimuthal(c, azimuthal(st[:, HALO + c], 0))
        return carry

    lax.fori_loop(0, count, own_part, 0)

    def far_part(c, carry):
        def step(d, inner):
            az_copy(d, c).wait_recv()
            add_azimuthal(c, azimuthal(other[d - 1, :, c], d))
            return inner

        return lax.fori_loop(1, n_az, step, carry)

    def axial_part(c, carry):
        along = axial(1, c)
        press = axial(4, c)
        speed = coef[0]
        ns[0, c] += speed * axial(0, c) + coef[2] * along
        ns[1, c] += speed * along + coef[4] * press
        ns[2, c] += speed * axial(2, c)
        ns[3, c] += speed * axial(3, c)
        ns[4, c] += speed * press + coef[3] * along
        return carry

    def out_copies(c):
        return (
            pltpu.make_async_copy(ns.at[:, c], out_section.at[:, c], out_sem.at[0, c]),
            pltpu.make_async_copy(nst.at[:, c], out_state.at[:, c], out_sem.at[1, c]),
        )

    def finish(c, carry):
        for f in range(5):
            nst[f, c] = st[f, HALO + c] + section_gain * ns[f, c]
        for copy in out_copies(c):
            copy.start()
        return carry

    early = count - 2
    lax.fori_loop(0, early, far_part, 0)

    def clear(start):
        st[:, pl.ds(start, HALO)] = jnp.zeros((5, HALO, rows, local), jnp.float32)

    pl.when(has_prev)(lambda: ax_copy(True).wait_recv())
    pl.when(has_next)(lambda: ax_copy(False).wait_recv())
    pl.when(jnp.logical_not(has_prev))(lambda: clear(0))
    pl.when(jnp.logical_not(has_next))(lambda: clear(count + HALO))
    lax.fori_loop(0, count, axial_part, 0)
    lax.fori_loop(0, early, finish, 0)
    lax.fori_loop(early, count, lambda c, carry: finish(c, far_part(c, carry)), 0)

    def drain(c, carry):
        for copy in out_copies(c):
            copy.wait()
        for d in range(1, n_az):
            az_copy(d, c).wait_send()
        return carry

    lax.fori_loop(0, count, drain, 0)
    pl.when(has_next)(lambda: ax_copy(True).wait_send())
    pl.when(has_prev)(lambda: ax_copy(False).wait_send())
    for k in range(2):
        pl.when(has_high)(lambda: rad_copy(True, k).wait_send())
        pl.when(has_low)(lambda: rad_copy(False, k).wait_send())


def body(mesh_sizes, state, section, mean_axial, mean_swirl, mean_density, sound_squared):
    n_ax, n_az, n_rad = mesh_sizes
    _, count, rows, local = state.shape
    table = jnp.asarray(spectral_tables(n_az, local))
    whole = (5, count, rows, local)
    far = pl.BlockSpec(memory_space=pltpu.HBM)
    f32 = jnp.float32
    dma = pltpu.SemaphoreType.DMA
    return pl.pallas_call(
        functools.partial(kernel, (n_ax, n_az, n_rad, count, rows, local)),
        out_shape=(jax.ShapeDtypeStruct(whole, f32), jax.ShapeDtypeStruct(whole, f32)),
        in_specs=[far] * 7,
        out_specs=(far, far),
        scratch_shapes=[
            pltpu.VMEM((5, count + 2 * HALO, rows, local), f32),
            pltpu.VMEM((2, count, rows + 2 * RIM, local), f32),
            pltpu.VMEM((n_az - 1, 5, count, rows, local), f32),
            pltpu.VMEM(whole, f32),
            pltpu.VMEM(whole, f32),
            pltpu.VMEM((8, rows, local), f32),
            pltpu.VMEM((n_az, 2, local, local), jnp.bfloat16),
            pltpu.VMEM((4, 1, rows), f32),
            dma((9,)),
            dma((n_az - 1, count)),
            dma((n_az - 1, count)),
            dma((2,)),
            dma((2,)),
            dma((2, 2)),
            dma((2, 2)),
            dma((2, count)),
        ],
        compiler_params=pltpu.CompilerParams(
            collective_id=0, has_side_effects=True, vmem_limit_bytes=48 * 2**20
        ),
        cost_estimate=pl.CostEstimate(
            flops=6 * 5 * count * rows * local * NT,
            bytes_accessed=4 * 4 * 5 * count * rows * local,
            transcendentals=0,
        ),
    )(
        state,
        section,
        mean_axial[None],
        mean_swirl[None],
        mean_density[None],
        sound_squared[None],
        table,
    )


def solution(mesh):
    spec = P(None, "ax", "rad", "az")
    sizes = (mesh.shape["ax"], mesh.shape["az"], mesh.shape["rad"])
    return jax.shard_map(
        functools.partial(body, sizes),
        mesh=mesh,
        in_specs=(spec, spec, P("rad"), P("rad"), P("rad"), P("rad")),
        out_specs=(spec, spec),
        check_vma=False,
    )
```

```python
import functools
import math

import jax
import jax.numpy as jnp
import numpy as np
from jax import lax
from jax.experimental import pallas as pl
from jax.experimental.pallas import tpu as pltpu
from jax.sharding import PartitionSpec as P

NT = 1024
MESH = pl.DeviceIdType.MESH

drp_coeffs = (0.770882380518, -0.166705904415, 0.02084314277)
section_keep = -0.4178904745
section_gain = 0.3792103129999
time_step = 0.25
HALO = 3
RIM = 8


def spectral_tables(owners, local):
    s = np.arange(local)[:, None]
    t = np.arange(local)[None, :]
    tables = []
    for d in range(owners):
        spacing = (t - s + d * local) % NT
        spacing = np.where(spacing > NT // 2, spacing - NT, spacing)
        angle = np.pi * spacing / NT
        safe = np.where(spacing == 0, 1.0, np.sin(angle))
        parity = 1.0 - 2.0 * (spacing % 2)
        tables.append(np.where(spacing == 0, 0.0, 0.5 * parity * np.cos(angle) / safe))
    full = np.stack(tables).astype(np.float32)
    high = full.astype(jnp.bfloat16)
    low = (full - high.astype(np.float32)).astype(jnp.bfloat16)
    return np.stack([high, low], axis=1)


def azimuthal(values, high_table, low_table):
    fields, rows, local = values.shape
    flat = values.reshape(fields * rows, local)
    high = flat.astype(jnp.bfloat16)
    low = (flat - high.astype(jnp.float32)).astype(jnp.bfloat16)
    dot = functools.partial(jnp.dot, preferred_element_type=jnp.float32)
    g = dot(high, high_table) + dot(low, high_table) + dot(high, low_table)
    return g.reshape(fields, rows, local)


def add_azimuthal(ns, coef, c, g):
    rate = coef[1]
    ns[0, c] += rate * g[0] + coef[5] * g[3]
    ns[1, c] += rate * g[1]
    ns[2, c] += rate * g[2]
    ns[3, c] += rate * g[3] + coef[7] * g[4]
    ns[4, c] += rate * g[4] + coef[6] * g[3]


def kernel(
    sizes, state, section, axial_speed, swirl, density_in, sound, table_in, ns, nst, late, coef,
    st, pr, other, table, means,
    load_sem, az_send, az_recv, ax_send, ax_recv, rad_send, rad_recv,
):
    n_ax, n_az, n_rad, count, rows, local = sizes
    ax = lax.axis_index("ax")
    az = lax.axis_index("az")
    rad = lax.axis_index("rad")
    has_prev, has_next = ax > 0, ax < n_ax - 1
    has_low, has_high = rad > 0, rad < n_rad - 1

    def az_copy(d, c, last=False):
        return pltpu.make_async_remote_copy(
            src_ref=state.at[:, c],
            dst_ref=late.at[d - 1] if last else other.at[d - 1, :, c],
            send_sem=az_send.at[d - 1, c],
            recv_sem=az_recv.at[d - 1, c],
            device_id={"az": lax.rem(az + d, n_az)},
            device_id_type=MESH,
        )

    def ax_copy(up):
        return pltpu.make_async_remote_copy(
            src_ref=state.at[:, pl.ds(count - HALO if up else 0, HALO)],
            dst_ref=st.at[:, pl.ds(0 if up else count + HALO, HALO)],
            send_sem=ax_send.at[0 if up else 1],
            recv_sem=ax_recv.at[0 if up else 1],
            device_id={"ax": ax + 1 if up else ax - 1},
            device_id_type=MESH,
        )

    def rad_copy(up, k):
        return pltpu.make_async_remote_copy(
            src_ref=state.at[2 + 2 * k, :, pl.ds(rows - RIM if up else 0, RIM)],
            dst_ref=pr.at[k, :, pl.ds(0 if up else rows + RIM, RIM)],
            send_sem=rad_send.at[0 if up else 1, k],
            recv_sem=rad_recv.at[0 if up else 1, k],
            device_id={"rad": rad + 1 if up else rad - 1},
            device_id_type=MESH,
        )

    loads = [
        pltpu.make_async_copy(state, st.at[:, pl.ds(HALO, count)], load_sem.at[0]),
        pltpu.make_async_copy(section, ns, load_sem.at[1]),
        pltpu.make_async_copy(state.at[2], pr.at[0, :, pl.ds(RIM, rows)], load_sem.at[2]),
        pltpu.make_async_copy(state.at[4], pr.at[1, :, pl.ds(RIM, rows)], load_sem.at[3]),
        pltpu.make_async_copy(table_in, table, load_sem.at[4]),
    ]
    vectors = [
        pltpu.make_async_copy(ref, means.at[i], load_sem.at[5 + i])
        for i, ref in enumerate((axial_speed, swirl, density_in, sound))
    ]
    for copy in vectors:
        copy.start()

    barrier = pltpu.get_barrier_semaphore()

    def greet(axis, index):
        pl.semaphore_signal(barrier, inc=1, device_id={axis: index}, device_id_type=MESH)

    for d in range(1, n_az):
        greet("az", lax.rem(az + d, n_az))
    pl.when(has_prev)(lambda: greet("ax", ax - 1))
    pl.when(has_next)(lambda: greet("ax", ax + 1))
    pl.when(has_low)(lambda: greet("rad", rad - 1))
    pl.when(has_high)(lambda: greet("rad", rad + 1))
    met = n_az - 1
    for there in (has_prev, has_next, has_low, has_high):
        met = met + there.astype(jnp.int32)
    pl.semaphore_wait(barrier, met)

    def send_plane(c, carry):
        for d in range(1, n_az):
            az_copy(d, c).start()
        return carry

    send_plane(0, 0)
    pl.when(has_next)(lambda: ax_copy(True).start())
    pl.when(has_prev)(lambda: ax_copy(False).start())
    for k in range(2):
        pl.when(has_high)(lambda: rad_copy(True, k).start())
        pl.when(has_low)(lambda: rad_copy(False, k).start())
    lax.fori_loop(1, count - 1, send_plane, 0)
    for d in range(1, n_az):
        az_copy(d, count - 1, True).start()
    for copy in loads:
        copy.start()

    for copy in vectors:
        copy.wait()

    pick = lax.broadcasted_iota(jnp.int32, (rows, rows), 0) == lax.broadcasted_iota(
        jnp.int32, (rows, rows), 1
    )

    def column(i):
        line = jnp.broadcast_to(means[i], (rows, rows))
        return jnp.sum(jnp.where(pick, line, 0.0), axis=1, keepdims=True)

    cell = lax.broadcasted_iota(jnp.int32, (rows, local), 0) + rad * rows
    inv_radius = 1.0 / (NT / (2.0 * math.pi) + cell.astype(jnp.float32) + 0.5)
    density = jnp.broadcast_to(column(2), (rows, local))
    minus = -time_step
    inverse = minus / density
    stiff = minus * density * column(3)
    coef[0] = jnp.broadcast_to(minus * column(0), (rows, local))
    coef[1] = minus * column(1) * inv_radius
    coef[2] = minus * density
    coef[3] = stiff
    coef[4] = inverse
    coef[5] = minus * density * inv_radius
    coef[6] = stiff * inv_radius
    coef[7] = inverse * inv_radius

    def radial(k, c):
        total = jnp.zeros((rows, local), jnp.float32)
        for j in range(1, 4):
            total += drp_coeffs[j - 1] * (
                pr[k, c, pl.ds(RIM + j, rows)] - pr[k, c, pl.ds(RIM - j, rows)]
            )
        return total

    def axial(f, c):
        total = jnp.zeros((rows, local), jnp.float32)
        for j in range(1, 4):
            total += drp_coeffs[j - 1] * (st[f, c + HALO + j] - st[f, c + HALO - j])
        return total

    for copy in loads:
        copy.wait()

    def wall(low):
        def fill(c, carry):
            for k, sign in enumerate((-1.0, 1.0)):
                for j in range(3):
                    if low:
                        pr[k, c, pl.ds(RIM - 1 - j, 1)] = sign * pr[k, c, pl.ds(RIM + j, 1)]
                    else:
                        pr[k, c, pl.ds(RIM + rows + j, 1)] = sign * pr[
                            k, c, pl.ds(RIM + rows - 1 - j, 1)
                        ]
            return carry

        lax.fori_loop(0, count, fill, 0)

    pl.when(jnp.logical_not(has_low))(lambda: wall(True))
    pl.when(jnp.logical_not(has_high))(lambda: wall(False))
    for k in range(2):
        pl.when(has_low)(lambda: rad_copy(True, k).wait_recv())
        pl.when(has_high)(lambda: rad_copy(False, k).wait_recv())

    def own_part(c, carry):
        for f in range(5):
            ns[f, c] = section_keep * ns[f, c]
        spread = radial(0, c)
        ns[0, c] += coef[2] * spread
        ns[4, c] += coef[3] * spread
        ns[2, c] += coef[4] * radial(1, c)
        add_azimuthal(ns, coef, c, azimuthal(st[:, HALO + c], table[0, 0], table[0, 1]))
        return carry

    lax.fori_loop(0, count, own_part, 0)

    def far_part(c, carry):
        def step(d, inner):
            az_copy(d, c).wait_recv()
            add_azimuthal(ns, coef, c, azimuthal(other[d - 1, :, c], table[d, 0], table[d, 1]))
            return inner

        return lax.fori_loop(1, n_az, step, carry)

    def axial_part(c, carry):
        along = axial(1, c)
        press = axial(4, c)
        speed = coef[0]
        ns[0, c] += speed * axial(0, c) + coef[2] * along
        ns[1, c] += speed * along + coef[4] * press
        ns[2, c] += speed * axial(2, c)
        ns[3, c] += speed * axial(3, c)
        ns[4, c] += speed * press + coef[3] * along
        return carry

    def finish(c, carry):
        for f in range(5):
            nst[f, c] = st[f, HALO + c] + section_gain * ns[f, c]
        return carry

    early = count - 2
    lax.fori_loop(0, early, far_part, 0)

    def clear(start):
        st[:, pl.ds(start, HALO)] = jnp.zeros((5, HALO, rows, local), jnp.float32)

    pl.when(has_prev)(lambda: ax_copy(True).wait_recv())
    pl.when(has_next)(lambda: ax_copy(False).wait_recv())
    pl.when(jnp.logical_not(has_prev))(lambda: clear(0))
    pl.when(jnp.logical_not(has_next))(lambda: clear(count + HALO))
    lax.fori_loop(0, count, axial_part, 0)
    lax.fori_loop(0, early, finish, 0)
    lax.fori_loop(early, count - 1, lambda c, carry: finish(c, far_part(c, carry)), 0)
    for f in range(5):
        nst[f, count - 1] = st[f, HALO + count - 1]

    def drain(c, carry):
        for d in range(1, n_az):
            az_copy(d, c).wait_send()
        return carry

    lax.fori_loop(0, count - 1, drain, 0)
    pl.when(has_next)(lambda: ax_copy(True).wait_send())
    pl.when(has_prev)(lambda: ax_copy(False).wait_send())
    for k in range(2):
        pl.when(has_high)(lambda: rad_copy(True, k).wait_send())
        pl.when(has_low)(lambda: rad_copy(False, k).wait_send())
    for d in range(1, n_az):
        az_copy(d, count - 1, True).wait_send()
        az_copy(d, count - 1, True).wait_recv()


def write_kernel(n_az, ns, nst, late, coef, table, out_state, out_section, fin, sem):
    last = ns.shape[1] - 1

    def copies(c):
        return (
            pltpu.make_async_copy(ns.at[:, c], out_section.at[:, c], sem.at[0, c]),
            pltpu.make_async_copy(nst.at[:, c], out_state.at[:, c], sem.at[1, c]),
        )

    def begin(c, carry):
        for copy in copies(c):
            copy.start()
        return carry

    def end(c, carry):
        for copy in copies(c):
            copy.wait()
        return carry

    lax.fori_loop(0, last, begin, 0)

    fin[:, 0] = ns[:, last]

    def far_part(d, carry):
        add_azimuthal(fin, coef, 0, azimuthal(late[d - 1], table[d, 0], table[d, 1]))
        return carry

    lax.fori_loop(1, n_az, far_part, 0)
    for f in range(5):
        fin[f, 1] = nst[f, last] + section_gain * fin[f, 0]
    ends = (
        pltpu.make_async_copy(fin.at[:, 0], out_section.at[:, last], sem.at[0, last]),
        pltpu.make_async_copy(fin.at[:, 1], out_state.at[:, last], sem.at[1, last]),
    )
    for copy in ends:
        copy.start()
    lax.fori_loop(0, last, end, 0)
    for copy in ends:
        copy.wait()


def body(mesh_sizes, state, section, mean_axial, mean_swirl, mean_density, sound_squared):
    n_ax, n_az, n_rad = mesh_sizes
    _, count, rows, local = state.shape
    table = jnp.asarray(spectral_tables(n_az, local))
    whole = (5, count, rows, local)
    late = (n_az - 1, 5, rows, local)
    coef = (8, rows, local)
    far = pl.BlockSpec(memory_space=pltpu.HBM)
    near = pl.BlockSpec(memory_space=pltpu.VMEM)
    f32 = jnp.float32
    dma = pltpu.SemaphoreType.DMA
    pin = functools.partial(pltpu.with_memory_space_constraint, memory_space=pltpu.HBM)
    ns, nst, late, coef = pl.pallas_call(
        functools.partial(kernel, (n_ax, n_az, n_rad, count, rows, local)),
        out_shape=tuple(pltpu.VMEM(shape, f32) for shape in (whole, whole, late, coef)),
        in_specs=[far] * 7,
        out_specs=(near,) * 4,
        scratch_shapes=[
            pltpu.VMEM((5, count + 2 * HALO, rows, local), f32),
            pltpu.VMEM((2, count, rows + 2 * RIM, local), f32),
            pltpu.VMEM((n_az - 1, 5, count - 1, rows, local), f32),
            pltpu.VMEM((n_az, 2, local, local), jnp.bfloat16),
            pltpu.VMEM((4, 1, rows), f32),
            dma((9,)),
            dma((n_az - 1, count)),
            dma((n_az - 1, count)),
            dma((2,)),
            dma((2,)),
            dma((2, 2)),
            dma((2, 2)),
        ],
        compiler_params=pltpu.CompilerParams(
            collective_id=0, has_side_effects=True, vmem_limit_bytes=28 * 2**20
        ),
        cost_estimate=pl.CostEstimate(
            flops=6 * 5 * count * rows * local * NT,
            bytes_accessed=4 * 4 * 5 * count * rows * local,
            transcendentals=0,
        ),
    )(
        pin(state),
        pin(section),
        pin(mean_axial[None]),
        pin(mean_swirl[None]),
        pin(mean_density[None]),
        pin(sound_squared[None]),
        pin(table),
    )
    return pl.pallas_call(
        functools.partial(write_kernel, n_az),
        out_shape=(jax.ShapeDtypeStruct(whole, f32), jax.ShapeDtypeStruct(whole, f32)),
        in_specs=[near] * 5,
        out_specs=(far, far),
        scratch_shapes=[pltpu.VMEM((5, 2, rows, local), f32), dma((2, count))],
        compiler_params=pltpu.CompilerParams(vmem_limit_bytes=8 * 2**20),
    )(ns, nst, late, coef, table)


def solution(mesh):
    spec = P(None, "ax", "rad", "az")
    sizes = (mesh.shape["ax"], mesh.shape["az"], mesh.shape["rad"])
    return jax.shard_map(
        functools.partial(body, sizes),
        mesh=mesh,
        in_specs=(spec, spec, P("rad"), P("rad"), P("rad"), P("rad")),
        out_specs=(spec, spec),
        check_vma=False,
    )
```

```python
import functools
import math

import jax
import jax.numpy as jnp
import numpy as np
from jax import lax
from jax.experimental import pallas as pl
from jax.experimental.pallas import tpu as pltpu
from jax.sharding import PartitionSpec as P

NT = 1024
MESH = pl.DeviceIdType.MESH

drp_coeffs = (0.770882380518, -0.166705904415, 0.02084314277)
section_keep = -0.4178904745
section_gain = 0.3792103129999
time_step = 0.25
HALO = 3
RIM = 8


def spectral_tables(owners, local):
    s = np.arange(local)[:, None]
    t = np.arange(local)[None, :]
    tables = []
    for d in range(owners):
        spacing = (t - s + d * local) % NT
        spacing = np.where(spacing > NT // 2, spacing - NT, spacing)
        angle = np.pi * spacing / NT
        safe = np.where(spacing == 0, 1.0, np.sin(angle))
        parity = 1.0 - 2.0 * (spacing % 2)
        tables.append(np.where(spacing == 0, 0.0, 0.5 * parity * np.cos(angle) / safe))
    full = np.stack(tables).astype(np.float32)
    high = full.astype(jnp.bfloat16)
    low = (full - high.astype(np.float32)).astype(jnp.bfloat16)
    return np.stack([high, low], axis=1)


def azimuthal(values, high_table, low_table):
    fields, rows, local = values.shape
    flat = values.reshape(fields * rows, local)
    high = flat.astype(jnp.bfloat16)
    low = (flat - high.astype(jnp.float32)).astype(jnp.bfloat16)
    dot = functools.partial(jnp.dot, preferred_element_type=jnp.float32)
    g = dot(high, high_table) + dot(low, high_table) + dot(high, low_table)
    return g.reshape(fields, rows, local)


def add_azimuthal(ns, coef, c, g):
    rate = coef[1]
    ns[0, c] += rate * g[0] + coef[5] * g[3]
    ns[1, c] += rate * g[1]
    ns[2, c] += rate * g[2]
    ns[3, c] += rate * g[3] + coef[7] * g[4]
    ns[4, c] += rate * g[4] + coef[6] * g[3]


def kernel(
    sizes, state, section, axial_speed, swirl, density_in, sound, table_in, ns, nst, late, coef,
    st, pr, other, table, means,
    load_sem, az_send, az_recv, ax_send, ax_recv, rad_send, rad_recv,
):
    n_ax, n_az, n_rad, count, rows, local = sizes
    ax = lax.axis_index("ax")
    az = lax.axis_index("az")
    rad = lax.axis_index("rad")
    has_prev, has_next = ax > 0, ax < n_ax - 1
    has_low, has_high = rad > 0, rad < n_rad - 1

    def az_copy(d, c, last=False):
        return pltpu.make_async_remote_copy(
            src_ref=state.at[:, c],
            dst_ref=late.at[d - 1] if last else other.at[d - 1, :, c],
            send_sem=az_send.at[d - 1, c],
            recv_sem=az_recv.at[d - 1, c],
            device_id={"az": lax.rem(az + d, n_az)},
            device_id_type=MESH,
        )

    def ax_copy(up):
        return pltpu.make_async_remote_copy(
            src_ref=state.at[:, pl.ds(count - HALO if up else 0, HALO)],
            dst_ref=st.at[:, pl.ds(0 if up else count + HALO, HALO)],
            send_sem=ax_send.at[0 if up else 1],
            recv_sem=ax_recv.at[0 if up else 1],
            device_id={"ax": ax + 1 if up else ax - 1},
            device_id_type=MESH,
        )

    def rad_copy(up, k):
        return pltpu.make_async_remote_copy(
            src_ref=state.at[2 + 2 * k, :, pl.ds(rows - RIM if up else 0, RIM)],
            dst_ref=pr.at[k, :, pl.ds(0 if up else rows + RIM, RIM)],
            send_sem=rad_send.at[0 if up else 1, k],
            recv_sem=rad_recv.at[0 if up else 1, k],
            device_id={"rad": rad + 1 if up else rad - 1},
            device_id_type=MESH,
        )

    loads = [
        pltpu.make_async_copy(state, st.at[:, pl.ds(HALO, count)], load_sem.at[0]),
        pltpu.make_async_copy(section, ns, load_sem.at[1]),
        pltpu.make_async_copy(state.at[2], pr.at[0, :, pl.ds(RIM, rows)], load_sem.at[2]),
        pltpu.make_async_copy(state.at[4], pr.at[1, :, pl.ds(RIM, rows)], load_sem.at[3]),
        pltpu.make_async_copy(table_in, table, load_sem.at[4]),
    ]
    vectors = [
        pltpu.make_async_copy(ref, means.at[i], load_sem.at[5 + i])
        for i, ref in enumerate((axial_speed, swirl, density_in, sound))
    ]

    barrier = pltpu.get_barrier_semaphore()

    def greet(axis, index):
        pl.semaphore_signal(barrier, inc=1, device_id={axis: index}, device_id_type=MESH)

    pl.when(has_prev)(lambda: greet("ax", ax - 1))
    pl.when(has_next)(lambda: greet("ax", ax + 1))
    for d in range(1, n_az):
        greet("az", lax.rem(az + d, n_az))
    pl.when(has_low)(lambda: greet("rad", rad - 1))
    pl.when(has_high)(lambda: greet("rad", rad + 1))
    for copy in vectors:
        copy.start()
    met = n_az - 1
    for there in (has_prev, has_next, has_low, has_high):
        met = met + there.astype(jnp.int32)
    pl.semaphore_wait(barrier, met)

    def send_plane(c, carry):
        for d in range(1, n_az):
            az_copy(d, c).start()
        return carry

    send_plane(0, 0)
    pl.when(has_next)(lambda: ax_copy(True).start())
    pl.when(has_prev)(lambda: ax_copy(False).start())
    for k in range(2):
        pl.when(has_high)(lambda: rad_copy(True, k).start())
        pl.when(has_low)(lambda: rad_copy(False, k).start())
    lax.fori_loop(1, count - 1, send_plane, 0)
    for d in range(1, n_az):
        az_copy(d, count - 1, True).start()
    for copy in loads:
        copy.start()

    for copy in vectors:
        copy.wait()

    pick = lax.broadcasted_iota(jnp.int32, (rows, rows), 0) == lax.broadcasted_iota(
        jnp.int32, (rows, rows), 1
    )

    def column(i):
        line = jnp.broadcast_to(means[i], (rows, rows))
        return jnp.sum(jnp.where(pick, line, 0.0), axis=1, keepdims=True)

    cell = lax.broadcasted_iota(jnp.int32, (rows, local), 0) + rad * rows
    inv_radius = 1.0 / (NT / (2.0 * math.pi) + cell.astype(jnp.float32) + 0.5)
    density = jnp.broadcast_to(column(2), (rows, local))
    minus = -time_step
    inverse = minus / density
    stiff = minus * density * column(3)
    coef[0] = jnp.broadcast_to(minus * column(0), (rows, local))
    coef[1] = minus * column(1) * inv_radius
    coef[2] = minus * density
    coef[3] = stiff
    coef[4] = inverse
    coef[5] = minus * density * inv_radius
    coef[6] = stiff * inv_radius
    coef[7] = inverse * inv_radius

    def radial(k, c):
        total = jnp.zeros((rows, local), jnp.float32)
        for j in range(1, 4):
            total += drp_coeffs[j - 1] * (
                pr[k, c, pl.ds(RIM + j, rows)] - pr[k, c, pl.ds(RIM - j, rows)]
            )
        return total

    def axial(f, c):
        total = jnp.zeros((rows, local), jnp.float32)
        for j in range(1, 4):
            total += drp_coeffs[j - 1] * (st[f, c + HALO + j] - st[f, c + HALO - j])
        return total

    for copy in loads:
        copy.wait()

    def wall(low):
        def fill(c, carry):
            for k, sign in enumerate((-1.0, 1.0)):
                for j in range(3):
                    if low:
                        pr[k, c, pl.ds(RIM - 1 - j, 1)] = sign * pr[k, c, pl.ds(RIM + j, 1)]
                    else:
                        pr[k, c, pl.ds(RIM + rows + j, 1)] = sign * pr[
                            k, c, pl.ds(RIM + rows - 1 - j, 1)
                        ]
            return carry

        lax.fori_loop(0, count, fill, 0)

    pl.when(jnp.logical_not(has_low))(lambda: wall(True))
    pl.when(jnp.logical_not(has_high))(lambda: wall(False))
    for k in range(2):
        pl.when(has_low)(lambda: rad_copy(True, k).wait_recv())
        pl.when(has_high)(lambda: rad_copy(False, k).wait_recv())

    def own_part(c, carry):
        for f in range(5):
            ns[f, c] = section_keep * ns[f, c]
        spread = radial(0, c)
        ns[0, c] += coef[2] * spread
        ns[4, c] += coef[3] * spread
        ns[2, c] += coef[4] * radial(1, c)
        add_azimuthal(ns, coef, c, azimuthal(st[:, HALO + c], table[0, 0], table[0, 1]))
        return carry

    lax.fori_loop(0, count, own_part, 0)

    def far_part(c, carry):
        def step(d, inner):
            az_copy(d, c).wait_recv()
            add_azimuthal(ns, coef, c, azimuthal(other[d - 1, :, c], table[d, 0], table[d, 1]))
            return inner

        return lax.fori_loop(1, n_az, step, carry)

    def axial_part(c, carry):
        along = axial(1, c)
        press = axial(4, c)
        speed = coef[0]
        ns[0, c] += speed * axial(0, c) + coef[2] * along
        ns[1, c] += speed * along + coef[4] * press
        ns[2, c] += speed * axial(2, c)
        ns[3, c] += speed * axial(3, c)
        ns[4, c] += speed * press + coef[3] * along
        return carry

    def finish(c, carry):
        for f in range(5):
            nst[f, c] = st[f, HALO + c] + section_gain * ns[f, c]
        return carry

    early = count - 2
    lax.fori_loop(0, early, far_part, 0)

    def clear(start):
        st[:, pl.ds(start, HALO)] = jnp.zeros((5, HALO, rows, local), jnp.float32)

    pl.when(has_prev)(lambda: ax_copy(True).wait_recv())
    pl.when(has_next)(lambda: ax_copy(False).wait_recv())
    pl.when(jnp.logical_not(has_prev))(lambda: clear(0))
    pl.when(jnp.logical_not(has_next))(lambda: clear(count + HALO))
    lax.fori_loop(0, count, axial_part, 0)
    lax.fori_loop(0, early, finish, 0)
    lax.fori_loop(early, count - 1, lambda c, carry: finish(c, far_part(c, carry)), 0)
    for f in range(5):
        nst[f, count - 1] = st[f, HALO + count - 1]

    def drain(c, carry):
        for d in range(1, n_az):
            az_copy(d, c).wait_send()
        return carry

    lax.fori_loop(0, count - 1, drain, 0)
    pl.when(has_next)(lambda: ax_copy(True).wait_send())
    pl.when(has_prev)(lambda: ax_copy(False).wait_send())
    for k in range(2):
        pl.when(has_high)(lambda: rad_copy(True, k).wait_send())
        pl.when(has_low)(lambda: rad_copy(False, k).wait_send())
    for d in range(1, n_az):
        az_copy(d, count - 1, True).wait_send()
        az_copy(d, count - 1, True).wait_recv()


def write_kernel(n_az, ns, nst, late, coef, table, out_state, out_section, fin, sem):
    last = ns.shape[1] - 1

    def copies(c):
        return (
            pltpu.make_async_copy(ns.at[:, c], out_section.at[:, c], sem.at[0, c]),
            pltpu.make_async_copy(nst.at[:, c], out_state.at[:, c], sem.at[1, c]),
        )

    def begin(c, carry):
        for copy in copies(c):
            copy.start()
        return carry

    def end(c, carry):
        for copy in copies(c):
            copy.wait()
        return carry

    lax.fori_loop(0, last, begin, 0)

    fin[:, 0] = ns[:, last]

    def far_part(d, carry):
        add_azimuthal(fin, coef, 0, azimuthal(late[d - 1], table[d, 0], table[d, 1]))
        return carry

    lax.fori_loop(1, n_az, far_part, 0)
    for f in range(5):
        fin[f, 1] = nst[f, last] + section_gain * fin[f, 0]
    ends = (
        pltpu.make_async_copy(fin.at[:, 0], out_section.at[:, last], sem.at[0, last]),
        pltpu.make_async_copy(fin.at[:, 1], out_state.at[:, last], sem.at[1, last]),
    )
    for copy in ends:
        copy.start()
    lax.fori_loop(0, last, end, 0)
    for copy in ends:
        copy.wait()


def body(mesh_sizes, state, section, mean_axial, mean_swirl, mean_density, sound_squared):
    n_ax, n_az, n_rad = mesh_sizes
    _, count, rows, local = state.shape
    table = jnp.asarray(spectral_tables(n_az, local))
    whole = (5, count, rows, local)
    late = (n_az - 1, 5, rows, local)
    coef = (8, rows, local)
    far = pl.BlockSpec(memory_space=pltpu.HBM)
    near = pl.BlockSpec(memory_space=pltpu.VMEM)
    f32 = jnp.float32
    dma = pltpu.SemaphoreType.DMA
    pin = functools.partial(pltpu.with_memory_space_constraint, memory_space=pltpu.HBM)
    ns, nst, late, coef = pl.pallas_call(
        functools.partial(kernel, (n_ax, n_az, n_rad, count, rows, local)),
        out_shape=tuple(pltpu.VMEM(shape, f32) for shape in (whole, whole, late, coef)),
        in_specs=[far] * 7,
        out_specs=(near,) * 4,
        scratch_shapes=[
            pltpu.VMEM((5, count + 2 * HALO, rows, local), f32),
            pltpu.VMEM((2, count, rows + 2 * RIM, local), f32),
            pltpu.VMEM((n_az - 1, 5, count - 1, rows, local), f32),
            pltpu.VMEM((n_az, 2, local, local), jnp.bfloat16),
            pltpu.VMEM((4, 1, rows), f32),
            dma((9,)),
            dma((n_az - 1, count)),
            dma((n_az - 1, count)),
            dma((2,)),
            dma((2,)),
            dma((2, 2)),
            dma((2, 2)),
        ],
        compiler_params=pltpu.CompilerParams(
            collective_id=0, has_side_effects=True, vmem_limit_bytes=28 * 2**20
        ),
        cost_estimate=pl.CostEstimate(
            flops=6 * 5 * count * rows * local * NT,
            bytes_accessed=4 * 4 * 5 * count * rows * local,
            transcendentals=0,
        ),
    )(
        pin(state),
        pin(section),
        pin(mean_axial[None]),
        pin(mean_swirl[None]),
        pin(mean_density[None]),
        pin(sound_squared[None]),
        pin(table),
    )
    return pl.pallas_call(
        functools.partial(write_kernel, n_az),
        out_shape=(jax.ShapeDtypeStruct(whole, f32), jax.ShapeDtypeStruct(whole, f32)),
        in_specs=[near] * 5,
        out_specs=(far, far),
        scratch_shapes=[pltpu.VMEM((5, 2, rows, local), f32), dma((2, count))],
        compiler_params=pltpu.CompilerParams(vmem_limit_bytes=8 * 2**20),
    )(ns, nst, late, coef, table)


def solution(mesh):
    spec = P(None, "ax", "rad", "az")
    sizes = (mesh.shape["ax"], mesh.shape["az"], mesh.shape["rad"])
    return jax.shard_map(
        functools.partial(body, sizes),
        mesh=mesh,
        in_specs=(spec, spec, P("rad"), P("rad"), P("rad"), P("rad")),
        out_specs=(spec, spec),
        check_vma=False,
    )
```
